32 devices in a mesh: gx: 8 (over y, x, core), gy: 4 (over z).
Axes of the slice: x: 2, y: 2, z: 4, core: 2. Of those that a mesh axis runs over, the one named last changes fastest.
Arguments:
- volume: bfloat16 [64, 4, 128, 2048], P(None, None, 'gy', 'gx'), may hold values from -6 to 6
- brick_mask: int32 [16, 64], P('gy', 'gx'), may hold values 0 or 1
- conv1_weight: bfloat16 [64, 64, 3, 3, 3], replicated, may hold values from -0.15625 to 0.15625
- conv1_bias: float32 [64], replicated, may hold values from -3 to 3
- conv2_weight: bfloat16 [64, 64, 1, 3, 3], replicated, may hold values from -0.25 to 0.25
- conv2_bias: float32 [64], replicated, may hold values from -3 to 3
- voxel_owner: int32 [262144, 1], P(('gx', 'gy')), may hold values from 0 to 31; in each aligned block of 8192 rows (0 to 8191, 8192 to 16383, ...) at most 512 rows name the same one
- voxel_segment: int32 [262144], P(('gx', 'gy')), may hold values from 0 to 127
Outputs:
- coarse: bfloat16 [64, 4, 64, 1024], P(None, None, 'gy', 'gx')
- supervox: float32 [64, 4096], P(None, ('gx', 'gy'))
The draws below stay inside these ranges and needn't reach their ends.
Inputs may be any that keep to these rules, and one draw needn't show every extreme that they name: `voxel_owner`: in the rows of one device no owner is named by more than 512 rows, a bound that some block reaches.
All inputs are finite; a program needn't handle non-finite values. No bound on the sum of `brick_mask` on one device may be relied on, other than what follows from the above.
Results may differ from the reference program's by a relative error of at most 0.0041.
Values may be sent and summed in bfloat16 or wider, within the bound.
A program may use at most 128 MiB of HBM per device.

```python
import math
import jax
import jax.numpy as jnp
import numpy as np
from jax import lax

C = 64
Z = 4
BY = 8
BX = 32
SEG_DEV = 128
NY = 128
NX = 2048
YC = 16
XC = 128
VOXC = 8192
CAPV = 512
SEGS = 4096
N_GX = 8
N_GY = 4
DEVICES = 32


def draw_voxel_segment(key, part):
    key = jax.random.fold_in(key, 7)
    values = jax.random.randint(key, (DEVICES * VOXC,), 0, SEG_DEV)
    values = values.at[0].set(0).at[1].set(SEG_DEV - 1)
    return values.astype(jnp.int32)


def set_ends(drawn, key, low, largest):
    longest = drawn.shape.index(max(drawn.shape))
    spots = []
    for shift in (0, 1):
        where = [jax.random.randint(jax.random.fold_in(key, axis), (), 0, length) for axis, length in enumerate(drawn.shape)]
        where[longest] = (where[longest] + shift) % drawn.shape[longest]
        spots.append(tuple(where))
    return drawn.at[spots[0]].set(low).at[spots[1]].set(largest)


def level_of(own_key, extent, split, smallest, high):
    level, own = 1.0, jax.random.fold_in(own_key, 6)
    for position, blocks in split:
        heights = jnp.exp(jax.random.uniform(jax.random.fold_in(own, position), (blocks,), jnp.float32, smallest / len(split), high / len(split)))
        level = level * jnp.repeat(heights, extent[position] // blocks).reshape([-1 if axis == position else 1 for axis in range(len(extent))])
    return level


def routed_block(key, own, number, rows, count, top, bound, slope):
    order = jax.random.permutation(key, count)
    packed, common = load_shares(count, rows * top, bound, slope, True), load_shares(count, rows * top, bound, slope, False)
    places = jnp.arange(count)

    def named(sizes, turn):
        used = int((sizes > 0).sum())
        fixed = max(1, used // 4)
        passed = fixed + (places - fixed + turn * (used - fixed)) % max(1, count - fixed)
        return jnp.zeros((count,), jnp.int32).at[order[jnp.where(places < fixed, places, passed)]].set(jnp.asarray(sizes, jnp.int32))

    sizes = jnp.where(number % 4 == 0, named(packed, number // 4), named(common, number - number // 4 - 1))
    mixed = jax.random.permutation(jax.random.fold_in(own, 3), count)
    donor, receiver = mixed[0:count // 2 * 2:2], mixed[1:count // 2 * 2:2]
    slack = jnp.minimum(sizes[donor] - 1, bound - sizes[receiver]) // 2
    slack = jnp.where((donor == order[0]) | (receiver == order[0]) | (sizes[receiver] == 0), 0, jnp.maximum(slack, 0))
    passed = jax.random.randint(jax.random.fold_in(own, 4), (count // 2,), 0, 1 << 20) % (slack + 1)
    sizes = sizes.at[donor].add(-passed).at[receiver].add(passed)
    labels = jnp.searchsorted(jnp.cumsum(sizes), jnp.arange(rows * top), side="right").astype(jnp.int32)
    listing = labels.reshape(top, rows).T
    listing = listing[jax.random.permutation(jax.random.fold_in(own, 1), rows)]
    turn = jax.random.randint(jax.random.fold_in(own, 2), (rows, 1), 0, top)
    return jnp.take_along_axis(listing, (jnp.arange(top)[None, :] + turn) % top, axis=1)


def load_shares(number_of, total, reach, skew, full):
    weights = [(1 << 20) // math.isqrt(standing ** skew) + 1 for standing in range(1, number_of + 1)]
    largest = reach if full else min(reach, max(-(-total // number_of), total * weights[0] // sum(weights)))
    least = 1 if total - largest >= number_of - 1 else 0
    counts, spare = [largest] + [least] * (number_of - 1), total - largest - least * (number_of - 1)
    while spare > 0:
        free = [i for i in range(1, number_of) if counts[i] < largest] or [i for i in range(1, number_of) if counts[i] < reach]
        mass, left = sum([weights[i] for i in free]), spare
        for i in free:
            addition = min(reach - counts[i], max(1, left * weights[i] // mass), spare)
            counts[i] = counts[i] + addition
            spare = spare - addition
    return np.array(counts)


def normal_values(own_key, shape, spread, most, shards=(), kind=jnp.bfloat16):
    gain = level_of(own_key, shape, shards, -0.22, 0.18) if shards else 1.0
    array = jax.random.normal(own_key, shape, jnp.float32) * spread * gain
    return jnp.minimum(jnp.maximum(array, -most), most).astype(kind)


def setup_inputs(seed: int = 0) -> dict:
    splits = jax.random.split(jax.random.key(seed), 9)
    volume = normal_values(splits[0], (C, Z, NY, NX), 1.0, 6.0, ((2, 4), (3, 8)))
    brick_mask = set_ends((jax.random.randint(splits[1], (NY // BY, NX // BX), 0, 4) < 3).astype(jnp.int32), jax.random.fold_in(splits[1], 1), 0, 1)
    conv1_weight = normal_values(splits[2], (C, C, 3, 3, 3), (27 * C) ** -0.5, 0.15625)
    conv1_bias = normal_values(splits[3], (C,), 0.5, 3.0, (), jnp.float32)
    conv2_weight = normal_values(splits[4], (C, C, 1, 3, 3), (9 * C) ** -0.5, 0.25)
    conv2_bias = normal_values(splits[5], (C,), 0.5, 3.0, (), jnp.float32)
    voxel_owner_keys = jax.random.split(jax.random.fold_in(splits[6], 1), (DEVICES * VOXC) // VOXC)
    voxel_owner_turns = jax.random.permutation(jax.random.fold_in(splits[6], 3), (DEVICES * VOXC) // VOXC)
    voxel_owner = jax.vmap(lambda own, number: routed_block(jax.random.fold_in(splits[6], 2), own, number, VOXC, DEVICES, 1, CAPV, 2))(voxel_owner_keys, voxel_owner_turns).reshape((DEVICES * VOXC, 1))
    voxel_segment = draw_voxel_segment(jax.random.fold_in(splits[8], 71), 0)
    return {"volume": volume, "brick_mask": brick_mask, "conv1_weight": conv1_weight, "conv1_bias": conv1_bias, "conv2_weight": conv2_weight, "conv2_bias": conv2_bias, "voxel_owner": voxel_owner, "voxel_segment": voxel_segment}


def reference(volume, brick_mask, conv1_weight, conv1_bias, conv2_weight, conv2_bias, voxel_owner, voxel_segment):
    voxel_mask = jnp.repeat(jnp.repeat(brick_mask, BY, 0), BX, 1).astype(jnp.bfloat16)
    masked = volume * voxel_mask[None, None]
    numbers = ('NCDHW', 'OIDHW', 'NCDHW')
    pre1 = lax.conv_general_dilated(masked[None], conv1_weight, (1, 1, 1), ((1, 1), (1, 1), (1, 1)), dimension_numbers=numbers, preferred_element_type=jnp.float32)[0]
    pre1 = pre1 + conv1_bias[:, None, None, None]
    hidden = (jnp.maximum(pre1, 0.0) * voxel_mask[None, None].astype(jnp.float32)).astype(jnp.bfloat16)
    pre2 = lax.conv_general_dilated(hidden[None], conv2_weight, (1, 2, 2), ((0, 0), (1, 1), (1, 1)), dimension_numbers=numbers, preferred_element_type=jnp.float32)[0]
    coarse = jnp.maximum(pre2 + conv2_bias[:, None, None, None], 0.0).astype(jnp.bfloat16)
    rows = coarse.reshape(C, Z, N_GY, YC, N_GX, XC).transpose(4, 2, 1, 3, 5, 0).reshape(DEVICES * VOXC, C)
    index = (voxel_owner[:, 0] * SEG_DEV + voxel_segment).astype(jnp.int32)
    sums = jax.ops.segment_sum(rows.astype(jnp.float32), index, num_segments=SEGS).T
    scale = lax.rsqrt(lax.optimization_barrier(jnp.mean(sums * sums, axis=0, keepdims=True)) + 1e-05)
    return (coarse, sums * scale)
```

```python
import jax
import jax.numpy as jnp
from jax import lax
from jax.sharding import PartitionSpec as P

BY = 8
BX = 32
SEG_DEV = 128


def halo(x, axis, dim, before, after):
    size, length = lax.axis_size(axis), x.shape[dim]
    up = [(i, i + 1) for i in range(size - 1)]
    down = [(i + 1, i) for i in range(size - 1)]
    first = lax.ppermute(lax.slice_in_dim(x, length - before, length, axis=dim), axis, up)
    parts = [first, x]
    if after:
        parts.append(lax.ppermute(lax.slice_in_dim(x, 0, after, axis=dim), axis, down))
    return jnp.concatenate(parts, axis=dim)


def per_device(volume, brick_mask, w1, b1, w2, b2, voxel_owner, voxel_segment):
    c, z, ny, nx = volume.shape
    bf16, f32 = jnp.bfloat16, jnp.float32
    mask = jnp.repeat(jnp.repeat(brick_mask, BY, 0), BX, 1).astype(bf16)
    masked = (volume * mask[None, None]).reshape(c * z, ny, nx)
    padded = halo(halo(masked, "gx", 2, 2, 1), "gy", 1, 2, 1)
    wide_mask = halo(halo(mask, "gx", 1, 1, 0), "gy", 0, 1, 0)
    offs = jnp.arange(z)[None, :] - jnp.arange(z)[:, None]
    band = jnp.stack([(offs == d - 1) for d in range(3)]).astype(bf16)
    w1b = jnp.einsum("ocdyx,dab->oacbyx", w1, band).reshape(c * z, c * z, 3, 3)
    w2b = jnp.einsum("ocyx,ab->oacbyx", w2[:, :, 0], jnp.eye(z, dtype=bf16)).reshape(
        c * z, c * z, 3, 3
    )
    numbers = ("NCHW", "OIHW", "NCHW")
    pre1 = lax.conv_general_dilated(
        padded[None], w1b, (1, 1), "VALID", dimension_numbers=numbers, preferred_element_type=f32
    )[0]
    pre1 = pre1 + jnp.repeat(b1, z)[:, None, None]
    hidden = (jnp.maximum(pre1, 0.0) * wide_mask.astype(f32)[None]).astype(bf16)
    pre2 = lax.conv_general_dilated(
        hidden[None], w2b, (2, 2), "VALID", dimension_numbers=numbers, preferred_element_type=f32
    )[0]
    coarse = jnp.maximum(pre2 + jnp.repeat(b2, z)[:, None, None], 0.0).astype(bf16)
    coarse = coarse.reshape(c, z, ny // 2, nx // 2)
    feats = coarse.reshape(c, -1)
    n = feats.shape[1]
    devices = lax.axis_size("gx") * lax.axis_size("gy")
    per = 2
    groups = devices // per
    owner = voxel_owner[:, 0]
    hi = owner // per
    col = (owner % per) * SEG_DEV + voxel_segment
    spread = jnp.where(
        hi[None, None, :] == jnp.arange(groups)[None, :, None], feats[:, None, :], jnp.zeros((), bf16)
    ).reshape(c * groups, n)
    hot = (col[:, None] == jnp.arange(per * SEG_DEV)[None, :]).astype(bf16)
    part = jnp.dot(spread, hot, preferred_element_type=f32).astype(bf16)
    part = part.reshape(c, devices, SEG_DEV)
    got = lax.all_to_all(part, ("gx", "gy"), split_axis=1, concat_axis=1, tiled=True)
    sums = jnp.sum(got.astype(f32), axis=1)
    scale = lax.rsqrt(jnp.mean(sums * sums, axis=0, keepdims=True) + 1e-05)
    return (coarse, sums * scale)


def solution(mesh):
    placed = (
        P(None, None, "gy", "gx"),
        P("gy", "gx"),
        P(),
        P(),
        P(),
        P(),
        P(("gx", "gy"), None),
        P(("gx", "gy")),
    )
    return jax.shard_map(
        per_device,
        mesh=mesh,
        in_specs=placed,
        out_specs=(P(None, None, "gy", "gx"), P(None, ("gx", "gy"))),
        check_vma=False,
    )
```

```python
import functools

import jax
import jax.numpy as jnp
from jax import lax
from jax.experimental import pallas as pl
from jax.experimental.pallas import tpu as pltpu
from jax.sharding import PartitionSpec as P

BY = 8
BX = 32
SEG_DEV = 128
PER = 2


def shift_in(block, axis, dim, before, after):
    size, length = lax.axis_size(axis), block.shape[dim]
    up = [(i, i + 1) for i in range(size - 1)]
    down = [(i + 1, i) for i in range(size - 1)]
    first = lax.ppermute(lax.slice_in_dim(block, length - before, length, axis=dim), axis, up)
    if not after:
        return first, None
    return first, lax.ppermute(lax.slice_in_dim(block, 0, after, axis=dim), axis, down)


def block_kernel(
    vol, mask, rows_halo, sides, column, wt1, wt2, b1, b2, row_mask, col_mask, hi, col,
    coarse, part,
    parted, src, hid, w1, w2, feats, flat, spread, hot, acc,
):
    f32, bf16 = jnp.float32, jnp.bfloat16
    c, z, ny, nx = vol.shape
    half = nx // 2
    cz = c * z
    depth = 3 * cz

    def dot(a, b):
        return jnp.dot(a, b, preferred_element_type=f32)

    w1[...] = jnp.zeros_like(w1)
    w2[...] = jnp.zeros_like(w2)
    for tap in range(9):
        for zo in range(z):
            for zi in range(max(0, zo - 1), min(z, zo + 2)):
                w1[pl.ds(zo * c, c), pl.ds(tap * cz + zi * c, c)] = wt1[(zi - zo + 1) * 9 + tap]
            w2[pl.ds(zo * c, c), pl.ds(tap * cz + zo * c, c)] = wt2[tap]

    at = lax.broadcasted_iota(jnp.int32, (nx, nx), 0)
    to = lax.broadcasted_iota(jnp.int32, (nx, nx), 1)
    sort = (at == jnp.where(to < half, 2 * to, 2 * to - nx + 1)).astype(f32).astype(bf16)
    lane = lax.broadcasted_iota(jnp.int32, (1, half), 1)

    def put_row(s, first, count, even, odd):
        left = pltpu.roll(sides[0, pl.ds(first, count), :], lax.rem(half - s, half), 1)
        right = pltpu.roll(sides[1, pl.ds(first, count), :], half - 1 - s, 1)
        odd_before = jnp.where(lane == 0, left, pltpu.roll(odd, 1, 1)).astype(bf16)
        even_after = jnp.where(lane == half - 1, right, pltpu.roll(even, half - 1, 1)).astype(bf16)
        even, odd = even.astype(bf16), odd.astype(bf16)
        for tap, pair in enumerate(((odd_before, even), (even, odd), (odd, even_after))):
            where = pl.ds(pl.multiple_of(s * depth + tap * cz + first, 64), count)
            src[where, pl.ds(0, half)] = pair[0]
            src[where, pl.ds(half, half)] = pair[1]

    for number, s in enumerate((0, 1, ny + 2)):
        for first in range(0, cz, c):
            both = dot(rows_halo[number, pl.ds(first, c), :], sort)
            put_row(s, first, c, both[:, :half], both[:, half:])
    for plane in range(z):
        block = (vol[:, plane] * mask[...][None]).reshape(c * ny, nx)
        both = dot(block, sort)
        parted[0] = both[:, :half]
        parted[1] = both[:, half:]

        @pl.loop(0, ny)
        def _(y):
            take = pl.ds(y, c, stride=ny)
            put_row(y + 2, plane * c, c, parted[0, take, :], parted[1, take, :])

    edge = dot(w1[...], column[...])
    edge = jnp.maximum(edge + b1[...], 0.0) * col_mask[...]

    def hidden_row(t, places):
        got = dot(w1[...], src[pl.ds(pl.multiple_of(t * depth, depth), 3 * depth), :])
        got = jnp.maximum(got + b1[...], 0.0)
        keep = row_mask[pl.ds(t, 1), :]
        even = got[:, :half] * keep
        odd = got[:, half:] * keep
        first = pltpu.roll(edge, lax.rem(half - t, half), 1)
        before = jnp.where(lane == 0, first, pltpu.roll(odd, 1, 1)).astype(bf16)
        parts = (before, even.astype(bf16), odd.astype(bf16))
        for p, dy, side in places:
            for tap in range(3):
                where = pl.multiple_of((p * 9 + dy * 3 + tap) * cz, cz)
                hid[pl.ds(where, cz), pl.ds(side * half, half)] = parts[tap]

    hidden_row(0, ((0, 0, 0),))

    @pl.loop(0, ny // 4)
    def _(p):
        t = 4 * p + 1
        hidden_row(t, ((p, 1, 0),))
        hidden_row(t + 1, ((p, 2, 0), (p, 0, 1)))
        hidden_row(t + 2, ((p, 1, 1),))
        hidden_row(t + 3, ((p, 2, 1), (p + 1, 0, 0)))
        got = dot(w2[...], hid[pl.ds(pl.multiple_of(p * 9 * cz, cz), 9 * cz), :])
        got = jnp.maximum(got + b2[...], 0.0).astype(bf16)
        feats[:, pl.ds(pl.multiple_of(p * nx, nx), nx)] = got
        wide = got.astype(f32)
        flat[pl.ds(2 * p, cz, stride=ny // 2), :] = wide[:, :half]
        flat[pl.ds(2 * p + 1, cz, stride=ny // 2), :] = wide[:, half:]

    for plane in range(z):
        piece = flat[pl.ds(plane * c * ny // 2, c * ny // 2), :]
        coarse[:, plane] = piece.reshape(c, ny // 2, half).astype(bf16)

    voxels = feats.shape[1]
    groups = part.shape[0] // PER
    chunk = spread.shape[0] // c

    @pl.loop(0, groups // chunk)
    def _(g):
        for plane in range(z):
            which = col[pl.ds(plane, 1), :]
            ids = lax.broadcasted_iota(jnp.int32, (PER * SEG_DEV, 1), 0)
            hot[...] = (ids == which).astype(f32).astype(bf16)
            owner = hi[pl.ds(plane, 1), :]
            for a in range(chunk):
                on = (owner == g * chunk + a).astype(f32).astype(bf16)
                spread[pl.ds(a * c, c), :] = feats[pl.ds(plane * c, c), :] * on
            got = lax.dot_general(
                spread[...], hot[...], (((1,), (1,)), ((), ())), preferred_element_type=f32
            )
            if plane == 0:
                acc[...] = got
            else:
                acc[...] += got
        for a in range(chunk):
            for n in range(PER):
                part[(g * chunk + a) * PER + n] = acc[
                    pl.ds(a * c, c), pl.ds(n * SEG_DEV, SEG_DEV)
                ].astype(bf16)


def per_device(volume, brick_mask, w1, b1, w2, b2, voxel_owner, voxel_segment):
    c, z, ny, nx = volume.shape
    bf16, f32 = jnp.bfloat16, jnp.float32
    half, cz = nx // 2, c * z
    devices = lax.axis_size("gx") * lax.axis_size("gy")
    mask = jnp.repeat(jnp.repeat(brick_mask, BY, 0), BX, 1).astype(bf16)

    def planes(y0, y1, x0, x1):
        return volume[:, :, y0:y1, x0:x1] * mask[None, None, y0:y1, x0:x1]

    up = [(i, i + 1) for i in range(lax.axis_size("gy") - 1)]
    down = [(i + 1, i) for i in range(lax.axis_size("gy") - 1)]
    above = lax.ppermute(planes(ny - 2, ny, 0, nx).transpose(2, 1, 0, 3), "gy", up)
    below = lax.ppermute(planes(0, 1, 0, nx).transpose(2, 1, 0, 3), "gy", down)
    rows_halo = jnp.concatenate([above, below]).reshape(3, cz, nx)

    def columns(x0, x1):
        mine = planes(0, ny, x0, x1).transpose(3, 1, 0, 2).reshape(x1 - x0, cz, ny)
        top = rows_halo[:2, :, x0:x1].transpose(2, 1, 0)
        return jnp.concatenate([mine, top, rows_halo[2:, :, x0:x1].transpose(2, 1, 0)], 2)

    left, right, own = columns(nx - 2, nx), columns(0, 1), columns(0, 1)
    right_way = [(i, i + 1) for i in range(lax.axis_size("gx") - 1)]
    left_way = [(i + 1, i) for i in range(lax.axis_size("gx") - 1)]
    left = lax.ppermute(left, "gx", right_way)
    right = lax.ppermute(right, "gx", left_way)
    lines = jnp.concatenate([left, own, right])
    lines = jnp.concatenate([lines[:, :, ny : ny + 2], lines[:, :, :ny], lines[:, :, ny + 2 :]], 2)
    lines = jnp.pad(lines, ((0, 0), (0, 0), (0, half - lines.shape[2] + 2)))
    column = jnp.concatenate([lines[:3, :, d : d + half].reshape(3 * cz, half) for d in range(3)])
    sides = jnp.stack([lines[1, :, :half], lines[3, :, :half]]).astype(f32)

    marks_y = lax.ppermute(brick_mask[-1:], "gy", up)
    bricks = jnp.concatenate([marks_y, brick_mask])
    marks_x = lax.ppermute(bricks[:, -1:], "gx", right_way)
    tall = jnp.concatenate([bricks[:1], jnp.repeat(bricks[1:], BY, 0)])
    row_mask = jnp.repeat(tall, BX // 2, 1).astype(f32)
    row_mask = jnp.pad(row_mask, ((0, 7), (0, 0)))
    col_mask = jnp.concatenate([marks_x[:1], jnp.repeat(marks_x[1:], BY, 0)]).astype(f32)
    col_mask = jnp.pad(col_mask.T, ((0, 0), (0, half - ny - 1)))

    wt1 = w1.transpose(2, 3, 4, 0, 1).reshape(27, c, c)
    wt2 = w2[:, :, 0].transpose(2, 3, 0, 1).reshape(9, c, c)
    tall1 = jnp.tile(b1, z)[:, None]
    tall2 = jnp.tile(b2, z)[:, None]
    owner = voxel_owner.reshape(z, -1)
    hi = owner // PER
    col = (owner % PER) * SEG_DEV + voxel_segment.reshape(z, -1)
    voxels = owner.shape[1]
    groups = devices // PER
    chunk = min(groups, 16)

    coarse, part = pl.pallas_call(
        block_kernel,
        out_shape=(
            jax.ShapeDtypeStruct((c, z, ny // 2, half), bf16),
            jax.ShapeDtypeStruct((devices, c, SEG_DEV), bf16),
        ),
        in_specs=[pl.BlockSpec(memory_space=pltpu.VMEM)] * 13,
        out_specs=[pl.BlockSpec(memory_space=pltpu.VMEM)] * 2,
        scratch_shapes=[
            pltpu.VMEM((2, c * ny, half), f32),
            pltpu.VMEM(((ny + 3) * 3 * cz, nx), bf16),
            pltpu.VMEM(((ny // 4 * 9 + 3) * cz, nx), bf16),
            pltpu.VMEM((cz, 9 * cz), bf16),
            pltpu.VMEM((cz, 9 * cz), bf16),
            pltpu.VMEM((cz, voxels), bf16),
            pltpu.VMEM((cz * ny // 2, half), f32),
            pltpu.VMEM((chunk * c, voxels), bf16),
            pltpu.VMEM((PER * SEG_DEV, voxels), bf16),
            pltpu.VMEM((chunk * c, PER * SEG_DEV), f32),
        ],
        compiler_params=pltpu.CompilerParams(vmem_limit_bytes=56 * 1024 * 1024),
    )(
        volume, mask, rows_halo, sides, column, wt1, wt2, tall1, tall2, row_mask, col_mask, hi, col
    )
    got = lax.all_to_all(part, ("gx", "gy"), split_axis=0, concat_axis=0, tiled=True)
    sums = jnp.sum(got.astype(f32), axis=0)
    scale = lax.rsqrt(jnp.mean(sums * sums, axis=0, keepdims=True) + 1e-05)
    return (coarse, sums * scale)


def solution(mesh):
    placed = (
        P(None, None, "gy", "gx"),
        P("gy", "gx"),
        P(),
        P(),
        P(),
        P(),
        P(("gx", "gy"), None),
        P(("gx", "gy")),
    )
    return jax.shard_map(
        per_device,
        mesh=mesh,
        in_specs=placed,
        out_specs=(P(None, None, "gy", "gx"), P(None, ("gx", "gy"))),
        check_vma=False,
    )
```

```python
import functools

import jax
import jax.numpy as jnp
from jax import lax
from jax.experimental import pallas as pl
from jax.experimental.pallas import tpu as pltpu
from jax.sharding import PartitionSpec as P

BY = 8
BX = 32
SEG_DEV = 128
PER = 2


def push(source, target, send, recv, axis, step):
    me, size = lax.axis_index(axis), lax.axis_size(axis)
    to = jnp.clip(me + step, 0, size - 1)
    has_to = (me + step >= 0) & (me + step < size)
    has_from = (me - step >= 0) & (me - step < size)
    copy = pltpu.make_async_remote_copy(
        src_ref=source, dst_ref=target, send_sem=send, recv_sem=recv,
        device_id={axis: to}, device_id_type=pl.DeviceIdType.MESH,
    )

    def start():
        @pl.when(has_to)
        def _():
            copy.start()

    def wait():
        @pl.when(has_to)
        def _():
            copy.wait_send()

        @pl.when(has_from)
        def _():
            copy.wait_recv()

    return start, wait


def greet():
    barrier = pltpu.get_barrier_semaphore()
    count = jnp.int32(0)
    for axis in ("gx", "gy"):
        me, size = lax.axis_index(axis), lax.axis_size(axis)
        for step in (-1, 1):
            there = (me + step >= 0) & (me + step < size)
            count = count + there.astype(jnp.int32)

            @pl.when(there)
            def _():
                pl.semaphore_signal(
                    barrier, inc=1, device_id={axis: jnp.clip(me + step, 0, size - 1)},
                    device_id_type=pl.DeviceIdType.MESH,
                )
    pl.semaphore_wait(barrier, count)


def block_kernel(
    vol, mask, wt1, wt2, bias1, bias2, own_mask, own_side, owners, segments,
    coarse, part,
    parted, src, hid, w1, w2, feats, flat, spread, hot, acc,
    halo, cols, cols_a, cols_b, got_a, got_b, sides, column, row_mask, top_mask, side_mask,
    left_mask, edge, send, recv,
):
    f32, bf16 = jnp.float32, jnp.bfloat16
    c, z, ny, nx = vol.shape
    half = nx // 2
    cz = c * z
    depth = 3 * cz

    def dot(a, b):
        return jnp.dot(a, b, preferred_element_type=f32)

    for ref in (halo, got_a, got_b, top_mask, left_mask, cols):
        ref[...] = jnp.zeros_like(ref)
    greet()

    at = lax.broadcasted_iota(jnp.int32, (nx, nx), 0)
    to = lax.broadcasted_iota(jnp.int32, (nx, nx), 1)
    sort = (at == jnp.where(to < half, 2 * to, 2 * to - nx + 1)).astype(f32).astype(bf16)
    lane = lax.broadcasted_iota(jnp.int32, (1, half), 1)

    def place(s, tap, first):
        return pl.ds(pl.multiple_of(s * depth + tap * cz + first, 64), c)

    def put_row(s, first, even, odd):
        here = pl.ds(first, c)
        there = lane == s
        last = lax.rem(s + 1, half)
        cols[0, here, :] = jnp.where(there, pltpu.roll(even, last, 1), cols[0, here, :])
        cols[1, here, :] = jnp.where(there, pltpu.roll(odd, last, 1), cols[1, here, :])
        cols[2, here, :] = jnp.where(there, pltpu.roll(even, s, 1), cols[2, here, :])
        even, odd = even.astype(bf16), odd.astype(bf16)
        src[place(s, 0, first), pl.ds(half, half)] = even
        src[place(s, 1, first), pl.ds(0, half)] = even
        src[place(s, 1, first), pl.ds(half, half)] = odd
        src[place(s, 2, first), pl.ds(0, half)] = odd

    def widen(s):
        for first in range(0, cz, c):
            even = src[place(s, 1, first), pl.ds(0, half)].astype(f32)
            odd = src[place(s, 1, first), pl.ds(half, half)].astype(f32)
            left = pltpu.roll(sides[0, pl.ds(first, c), :], lax.rem(half - s, half), 1)
            right = pltpu.roll(sides[1, pl.ds(first, c), :], half - 1 - s, 1)
            before = jnp.where(lane == 0, left, pltpu.roll(odd, 1, 1))
            after = jnp.where(lane == half - 1, right, pltpu.roll(even, half - 1, 1))
            src[place(s, 0, first), pl.ds(0, half)] = before.astype(bf16)
            src[place(s, 2, first), pl.ds(half, half)] = after.astype(bf16)

    for plane in range(z):
        block = (vol[:, plane] * mask[...][None]).reshape(c * ny, nx)
        both = dot(block, sort)
        parted[0] = both[:, :half]
        parted[1] = both[:, half:]

        @pl.loop(0, ny)
        def _(y):
            take = pl.ds(y, c, stride=ny)
            put_row(y + 2, plane * c, parted[0, take, :], parted[1, take, :])

    def line(s):
        return src.at[pl.ds(s * depth + cz, cz), :]

    rows = [
        push(line(ny), halo.at[0], send.at[0], recv.at[0], "gy", 1),
        push(line(ny + 1), halo.at[1], send.at[1], recv.at[1], "gy", 1),
        push(line(2), halo.at[2], send.at[2], recv.at[2], "gy", -1),
        push(own_mask.at[pl.ds(ny - 8, 8), :], top_mask, send.at[3], recv.at[3], "gy", 1),
    ]
    cols_a[...] = cols[...].astype(bf16)
    near = [
        push(cols_a.at[1], got_a.at[0], send.at[4], recv.at[4], "gx", 1),
        push(cols_a.at[2], got_a.at[1], send.at[5], recv.at[5], "gx", -1),
    ]
    for start, wait in near + rows:
        start()

    w1[...] = jnp.zeros_like(w1)
    w2[...] = jnp.zeros_like(w2)
    for tap in range(9):
        for zo in range(z):
            for zi in range(max(0, zo - 1), min(z, zo + 2)):
                w1[pl.ds(zo * c, c), pl.ds(tap * cz + zi * c, c)] = wt1[(zi - zo + 1) * 9 + tap]
            w2[pl.ds(zo * c, c), pl.ds(tap * cz + zo * c, c)] = wt2[tap]
    b1 = jnp.concatenate([bias1[...]] * z, 0)
    b2 = jnp.concatenate([bias2[...]] * z, 0)
    row_mask[pl.ds(1, ny), :] = own_mask[...]

    for start, wait in near:
        wait()
    sides[...] = got_a[...].astype(f32)

    @pl.loop(2, ny + 2)
    def _(s):
        widen(s)

    def hidden_row(t, places):
        got = dot(w1[...], src[pl.ds(pl.multiple_of(t * depth, depth), 3 * depth), :])
        got = jnp.maximum(got + b1, 0.0)
        keep = row_mask[pl.ds(t, 1), :]
        even = got[:, :half] * keep
        odd = got[:, half:] * keep
        parts = (pltpu.roll(odd, 1, 1).astype(bf16), even.astype(bf16), odd.astype(bf16))
        for p, dy, side in places:
            for tap in range(3):
                where = pl.multiple_of((p * 9 + dy * 3 + tap) * cz, cz)
                hid[pl.ds(where, cz), pl.ds(side * half, half)] = parts[tap]

    def four_rows(p):
        t = 4 * p + 1
        hidden_row(t, ((p, 1, 0),))
        hidden_row(t + 1, ((p, 2, 0), (p, 0, 1)))
        hidden_row(t + 2, ((p, 1, 1),))
        hidden_row(t + 3, ((p, 2, 1), (p + 1, 0, 0)))

    quads = ny // 4

    @pl.loop(1, quads // 2 + 1)
    def _(p):
        four_rows(p)

    for start, wait in rows:
        wait()
    for number, s in enumerate((0, 1, ny + 2)):
        for first in range(0, cz, c):
            both = halo[number, pl.ds(first, c), :].astype(f32)
            put_row(s, first, both[:, :half], both[:, half:])
    row_mask[pl.ds(0, 1), :] = top_mask[pl.ds(7, 1), :]
    cols_b[...] = cols[...].astype(bf16)
    side_mask[...] = jnp.where(
        lane == 0, pltpu.roll(jnp.broadcast_to(top_mask[pl.ds(7, 1), :], (8, half)), 1, 1),
        own_side[...],
    )
    far = [
        push(cols_b.at[pl.ds(0, 2)], got_b.at[pl.ds(0, 2)], send.at[6], recv.at[6], "gx", 1),
        push(cols_b.at[2], got_b.at[2], send.at[7], recv.at[7], "gx", -1),
        push(side_mask, left_mask, send.at[8], recv.at[8], "gx", 1),
    ]
    for start, wait in far:
        start()

    @pl.loop(quads // 2 + 1, quads - 1)
    def _(p):
        four_rows(p)

    for start, wait in far:
        wait()
    sides[...] = got_b[pl.ds(1, 2)].astype(f32)
    for s in (0, 1, ny + 2):
        widen(s)

    for dx in range(3):
        wide = cols[2] if dx == 2 else got_b[dx].astype(f32)
        for dy in range(3):
            moved = wide if dy == 0 else pltpu.roll(wide, half - dy, 1)
            column[pl.ds((dy * 3 + dx) * cz, cz), :] = moved.astype(bf16)
    got = dot(w1[...], column[...])
    edge[...] = jnp.maximum(got + b1, 0.0) * left_mask[pl.ds(0, 1), :]
    hidden_row(0, ((0, 0, 0),))

    @pl.loop(0, 2)
    def _(i):
        four_rows(i * (quads - 1))

    @pl.loop(0, quads)
    def _(p):
        for dy in range(3):
            for side in range(2):
                t = 4 * p + 2 * side + dy
                spot = pl.ds(pl.multiple_of((p * 9 + dy * 3) * cz, cz), cz)
                first = pltpu.roll(edge[...], lax.rem(half - t, half), 1)
                old = hid[spot, pl.ds(side * half, half)].astype(f32)
                hid[spot, pl.ds(side * half, half)] = jnp.where(lane == 0, first, old).astype(bf16)
        got = dot(w2[...], hid[pl.ds(pl.multiple_of(p * 9 * cz, cz), 9 * cz), :])
        got = jnp.maximum(got + b2, 0.0).astype(bf16)
        feats[:, pl.ds(pl.multiple_of(p * nx, nx), nx)] = got
        wide = got.astype(f32)
        flat[pl.ds(2 * p, cz, stride=ny // 2), :] = wide[:, :half]
        flat[pl.ds(2 * p + 1, cz, stride=ny // 2), :] = wide[:, half:]

    for plane in range(z):
        piece = flat[pl.ds(plane * c * ny // 2, c * ny // 2), :]
        coarse[:, plane] = piece.reshape(c, ny // 2, half).astype(bf16)

    voxels = feats.shape[1]
    groups = part.shape[0] // PER
    chunk = spread.shape[0] // c

    @pl.loop(0, groups // chunk)
    def _(g):
        for plane in range(z):
            which = lax.rem(owners[pl.ds(plane, 1), :], PER) * SEG_DEV + segments[pl.ds(plane, 1), :]
            ids = lax.broadcasted_iota(jnp.int32, (PER * SEG_DEV, 1), 0)
            hot[...] = (ids == which).astype(f32).astype(bf16)
            owner = owners[pl.ds(plane, 1), :] // PER
            for a in range(chunk):
                on = (owner == g * chunk + a).astype(f32).astype(bf16)
                spread[pl.ds(a * c, c), :] = feats[pl.ds(plane * c, c), :] * on
            got = lax.dot_general(
                spread[...], hot[...], (((1,), (1,)), ((), ())), preferred_element_type=f32
            )
            if plane == 0:
                acc[...] = got
            else:
                acc[...] += got
        for a in range(chunk):
            for n in range(PER):
                part[(g * chunk + a) * PER + n] = acc[
                    pl.ds(a * c, c), pl.ds(n * SEG_DEV, SEG_DEV)
                ].astype(bf16)


def reduce_kernel(part, out, mine, got_x, got_y, send_x, recv_x, send_y, recv_y):
    f32, bf16 = jnp.float32, jnp.bfloat16
    x, y = lax.axis_index("gx"), lax.axis_index("gy")
    size_x, size_y = lax.axis_size("gx"), lax.axis_size("gy")
    barrier = pltpu.get_barrier_semaphore()
    for i in range(1, size_x):
        pl.semaphore_signal(
            barrier, inc=1, device_id={"gx": lax.rem(x + i, size_x)},
            device_id_type=pl.DeviceIdType.MESH,
        )
    for i in range(1, size_y):
        pl.semaphore_signal(
            barrier, inc=1, device_id={"gy": lax.rem(y + i, size_y)},
            device_id_type=pl.DeviceIdType.MESH,
        )
    pl.semaphore_wait(barrier, size_x + size_y - 2)

    def spread(axis, me, size, source, target, send, recv):
        copies = []
        for i in range(1, size):
            to = lax.rem(me + i, size)
            copy = pltpu.make_async_remote_copy(
                src_ref=source.at[to], dst_ref=target.at[i], send_sem=send.at[i],
                recv_sem=recv.at[i], device_id={axis: to},
                device_id_type=pl.DeviceIdType.MESH,
            )
            copy.start()
            copies.append(copy)
        for copy in copies:
            copy.wait()

    spread("gx", x, size_x, part, got_x, send_x, recv_x)
    total = part[x].astype(f32)
    for i in range(1, size_x):
        total = total + got_x[i].astype(f32)
    mine[...] = total.astype(bf16)
    spread("gy", y, size_y, mine, got_y, send_y, recv_y)
    sums = mine[y].astype(f32)
    for i in range(1, size_y):
        sums = sums + got_y[i].astype(f32)
    out[...] = sums * lax.rsqrt(jnp.mean(sums * sums, axis=0, keepdims=True) + 1e-05)


def per_device(volume, brick_mask, w1, b1, w2, b2, voxel_owner, voxel_segment):
    c, z, ny, nx = volume.shape
    bf16, f32 = jnp.bfloat16, jnp.float32
    half, cz = nx // 2, c * z
    size_x, size_y = lax.axis_size("gx"), lax.axis_size("gy")
    devices = size_x * size_y
    tall = jnp.repeat(brick_mask, BY, 0)
    mask = jnp.repeat(tall, BX, 1).astype(bf16)
    own_mask = jnp.repeat(tall, BX // 2, 1).astype(f32)
    own_side = jnp.pad(tall[:, -1], (1, half - ny - 1)).astype(f32)
    own_side = jnp.broadcast_to(own_side[None], (8, half))
    wt1 = w1.transpose(2, 3, 4, 0, 1).reshape(27, c, c)
    wt2 = w2[:, :, 0].transpose(2, 3, 0, 1).reshape(9, c, c)
    owner = voxel_owner.reshape(z, -1)
    segment = voxel_segment.reshape(z, -1)
    voxels = owner.shape[1]
    groups = devices // PER
    chunk = min(groups, 16)

    coarse, part = pl.pallas_call(
        block_kernel,
        out_shape=(
            jax.ShapeDtypeStruct((c, z, ny // 2, half), bf16),
            jax.ShapeDtypeStruct((devices, c, SEG_DEV), bf16),
        ),
        in_specs=[pl.BlockSpec(memory_space=pltpu.VMEM)] * 10,
        out_specs=[pl.BlockSpec(memory_space=pltpu.VMEM)] * 2,
        scratch_shapes=[
            pltpu.VMEM((2, c * ny, half), f32),
            pltpu.VMEM(((ny + 3) * 3 * cz, nx), bf16),
            pltpu.VMEM(((ny // 4 * 9 + 3) * cz, nx), bf16),
            pltpu.VMEM((cz, 9 * cz), bf16),
            pltpu.VMEM((cz, 9 * cz), bf16),
            pltpu.VMEM((cz, voxels), bf16),
            pltpu.VMEM((cz * ny // 2, half), f32),
            pltpu.VMEM((chunk * c, voxels), bf16),
            pltpu.VMEM((PER * SEG_DEV, voxels), bf16),
            pltpu.VMEM((chunk * c, PER * SEG_DEV), f32),
            pltpu.VMEM((3, cz, nx), bf16),
            pltpu.VMEM((3, cz, half), f32),
            pltpu.VMEM((3, cz, half), bf16),
            pltpu.VMEM((3, cz, half), bf16),
            pltpu.VMEM((2, cz, half), bf16),
            pltpu.VMEM((3, cz, half), bf16),
            pltpu.VMEM((2, cz, half), f32),
            pltpu.VMEM((9 * cz, half), bf16),
            pltpu.VMEM((ny + 8, half), f32),
            pltpu.VMEM((8, half), f32),
            pltpu.VMEM((8, half), f32),
            pltpu.VMEM((8, half), f32),
            pltpu.VMEM((cz, half), f32),
            pltpu.SemaphoreType.DMA((9,)),
            pltpu.SemaphoreType.DMA((9,)),
        ],
        compiler_params=pltpu.CompilerParams(
            collective_id=0, has_side_effects=True, vmem_limit_bytes=58 * 1024 * 1024
        ),
    )(volume, mask, wt1, wt2, b1[:, None], b2[:, None], own_mask, own_side, owner, segment)
    supervox = pl.pallas_call(
        reduce_kernel,
        out_shape=jax.ShapeDtypeStruct((c, SEG_DEV), f32),
        in_specs=[pl.BlockSpec(memory_space=pltpu.VMEM)],
        out_specs=pl.BlockSpec(memory_space=pltpu.VMEM),
        scratch_shapes=[
            pltpu.VMEM((size_y, c, SEG_DEV), bf16),
            pltpu.VMEM((size_x, size_y, c, SEG_DEV), bf16),
            pltpu.VMEM((size_y, c, SEG_DEV), bf16),
            pltpu.SemaphoreType.DMA((size_x,)),
            pltpu.SemaphoreType.DMA((size_x,)),
            pltpu.SemaphoreType.DMA((size_y,)),
            pltpu.SemaphoreType.DMA((size_y,)),
        ],
        compiler_params=pltpu.CompilerParams(
            collective_id=1, has_side_effects=True, vmem_limit_bytes=32 * 1024 * 1024
        ),
    )(part.reshape(size_x, size_y, c, SEG_DEV))
    return (coarse, supervox)


def solution(mesh):
    placed = (
        P(None, None, "gy", "gx"),
        P("gy", "gx"),
        P(),
        P(),
        P(),
        P(),
        P(("gx", "gy"), None),
        P(("gx", "gy")),
    )
    return jax.shard_map(
        per_device,
        mesh=mesh,
        in_specs=placed,
        out_specs=(P(None, None, "gy", "gx"), P(None, ("gx", "gy"))),
        check_vma=False,
    )
```

```python
import functools

import jax
import jax.numpy as jnp
from jax import lax
from jax.experimental import pallas as pl
from jax.experimental.pallas import tpu as pltpu
from jax.sharding import PartitionSpec as P

BY = 8
BX = 32
SEG_DEV = 128
PER = 2


def push(source, target, send, recv, axis, step):
    me, size = lax.axis_index(axis), lax.axis_size(axis)
    to = jnp.clip(me + step, 0, size - 1)
    has_to = (me + step >= 0) & (me + step < size)
    has_from = (me - step >= 0) & (me - step < size)
    copy = pltpu.make_async_remote_copy(
        src_ref=source, dst_ref=target, send_sem=send, recv_sem=recv,
        device_id={axis: to}, device_id_type=pl.DeviceIdType.MESH,
    )

    def start():
        @pl.when(has_to)
        def _():
            copy.start()

    def wait():
        @pl.when(has_to)
        def _():
            copy.wait_send()

        @pl.when(has_from)
        def _():
            copy.wait_recv()

    return start, wait


def greet():
    barrier = pltpu.get_barrier_semaphore()
    count = jnp.int32(0)
    for axis in ("gx", "gy"):
        me, size = lax.axis_index(axis), lax.axis_size(axis)
        for step in (-1, 1):
            there = (me + step >= 0) & (me + step < size)
            count = count + there.astype(jnp.int32)

            @pl.when(there)
            def _():
                pl.semaphore_signal(
                    barrier, inc=1, device_id={axis: jnp.clip(me + step, 0, size - 1)},
                    device_id_type=pl.DeviceIdType.MESH,
                )
    pl.semaphore_wait(barrier, count)


def block_kernel(
    vol, mask, wt1, wt2, bias1, bias2, own_mask, own_side, owners, segments,
    coarse, part,
    parted, src, hid, w1, w2, feats, flat, spread, hot, acc,
    halo, cols, cols_a, cols_b, got_a, got_b, sides, column, row_mask, top_mask, side_mask,
    left_mask, edge, send, recv,
):
    f32, bf16 = jnp.float32, jnp.bfloat16
    c, z, ny, nx = vol.shape
    half = nx // 2
    cz = c * z
    depth = 3 * cz

    def dot(a, b):
        return jnp.dot(a, b, preferred_element_type=f32)

    for ref in (halo, got_a, got_b, top_mask, left_mask, cols):
        ref[...] = jnp.zeros_like(ref)
    greet()

    at = lax.broadcasted_iota(jnp.int32, (nx, nx), 0)
    to = lax.broadcasted_iota(jnp.int32, (nx, nx), 1)
    sort = (at == jnp.where(to < half, 2 * to, 2 * to - nx + 1)).astype(f32).astype(bf16)
    lane = lax.broadcasted_iota(jnp.int32, (1, half), 1)

    def place(s, tap, first):
        return pl.ds(pl.multiple_of(s * depth + tap * cz + first, 64), c)

    def put_row(s, first, even, odd):
        here = pl.ds(first, c)
        there = lane == s
        last = lax.rem(s + 1, half)
        cols[0, here, :] = jnp.where(there, pltpu.roll(even, last, 1), cols[0, here, :])
        cols[1, here, :] = jnp.where(there, pltpu.roll(odd, last, 1), cols[1, here, :])
        cols[2, here, :] = jnp.where(there, pltpu.roll(even, s, 1), cols[2, here, :])
        even, odd = even.astype(bf16), odd.astype(bf16)
        src[place(s, 0, first), pl.ds(half, half)] = even
        src[place(s, 1, first), pl.ds(0, half)] = even
        src[place(s, 1, first), pl.ds(half, half)] = odd
        src[place(s, 2, first), pl.ds(0, half)] = odd

    def widen(s):
        base = s * depth
        middle = pl.ds(pl.multiple_of(base + cz, cz), cz)
        even = src[middle, pl.ds(0, half)].astype(f32)
        odd = src[middle, pl.ds(half, half)].astype(f32)
        left = pltpu.roll(sides[0], lax.rem(half - s, half), 1)
        right = pltpu.roll(sides[1], half - 1 - s, 1)
        before = jnp.where(lane == 0, left, pltpu.roll(odd, 1, 1))
        after = jnp.where(lane == half - 1, right, pltpu.roll(even, half - 1, 1))
        src[pl.ds(pl.multiple_of(base, cz), cz), pl.ds(0, half)] = before.astype(bf16)
        src[pl.ds(pl.multiple_of(base + 2 * cz, cz), cz), pl.ds(half, half)] = after.astype(bf16)

    for plane in range(z):
        block = (vol[:, plane] * mask[...][None]).reshape(c * ny, nx)
        both = dot(block, sort)
        parted[0] = both[:, :half]
        parted[1] = both[:, half:]

        @pl.loop(0, ny, unroll=4)
        def _(y):
            take = pl.ds(y, c, stride=ny)
            put_row(y + 2, plane * c, parted[0, take, :], parted[1, take, :])

    def line(s):
        return src.at[pl.ds(s * depth + cz, cz), :]

    rows = [
        push(line(ny), halo.at[0], send.at[0], recv.at[0], "gy", 1),
        push(line(ny + 1), halo.at[1], send.at[1], recv.at[1], "gy", 1),
        push(line(2), halo.at[2], send.at[2], recv.at[2], "gy", -1),
        push(own_mask.at[pl.ds(ny - 8, 8), :], top_mask, send.at[3], recv.at[3], "gy", 1),
    ]
    cols_a[...] = cols[...].astype(bf16)
    near = [
        push(cols_a.at[1], got_a.at[0], send.at[4], recv.at[4], "gx", 1),
        push(cols_a.at[2], got_a.at[1], send.at[5], recv.at[5], "gx", -1),
    ]
    for start, wait in near + rows:
        start()

    w1[...] = jnp.zeros_like(w1)
    w2[...] = jnp.zeros_like(w2)
    for tap in range(9):
        for zo in range(z):
            for zi in range(max(0, zo - 1), min(z, zo + 2)):
                w1[pl.ds(zo * c, c), pl.ds(tap * cz + zi * c, c)] = wt1[(zi - zo + 1) * 9 + tap]
            w2[pl.ds(zo * c, c), pl.ds(tap * cz + zo * c, c)] = wt2[tap]
    row = lax.broadcasted_iota(jnp.int32, (c, c), 0)
    diagonal = row == lax.broadcasted_iota(jnp.int32, (c, c), 1)
    b1, b2 = [
        jnp.concatenate([jnp.sum(jnp.where(diagonal, bias[...], 0.0), 1, keepdims=True)] * z, 0)
        for bias in (bias1, bias2)
    ]
    row_mask[pl.ds(1, ny), :] = own_mask[...]

    for start, wait in near:
        wait()
    sides[...] = got_a[...].astype(f32)

    @pl.loop(2, ny + 2)
    def _(s):
        widen(s)

    def hidden_row(t, places):
        got = dot(w1[...], src[pl.ds(pl.multiple_of(t * depth, depth), 3 * depth), :])
        got = jnp.maximum(got + b1, 0.0)
        keep = row_mask[pl.ds(t, 1), :]
        even = got[:, :half] * keep
        odd = got[:, half:] * keep
        parts = (pltpu.roll(odd, 1, 1).astype(bf16), even.astype(bf16), odd.astype(bf16))
        for p, dy, side in places:
            for tap in range(3):
                where = pl.multiple_of((p * 9 + dy * 3 + tap) * cz, cz)
                hid[pl.ds(where, cz), pl.ds(side * half, half)] = parts[tap]

    def four_rows(p):
        t = 4 * p + 1
        hidden_row(t, ((p, 1, 0),))
        hidden_row(t + 1, ((p, 2, 0), (p, 0, 1)))
        hidden_row(t + 2, ((p, 1, 1),))
        hidden_row(t + 3, ((p, 2, 1), (p + 1, 0, 0)))

    quads = ny // 4

    @pl.loop(1, quads // 2 + 1)
    def _(p):
        four_rows(p)

    for start, wait in rows:
        wait()
    for number, s in enumerate((0, 1, ny + 2)):
        for first in range(0, cz, c):
            both = halo[number, pl.ds(first, c), :].astype(f32)
            put_row(s, first, both[:, :half], both[:, half:])
    row_mask[pl.ds(0, 1), :] = top_mask[pl.ds(7, 1), :]
    cols_b[...] = cols[...].astype(bf16)
    side_mask[...] = jnp.where(
        lane == 0, pltpu.roll(jnp.broadcast_to(top_mask[pl.ds(7, 1), :], (8, half)), 1, 1),
        own_side[...],
    )
    far = [
        push(cols_b.at[pl.ds(0, 2)], got_b.at[pl.ds(0, 2)], send.at[6], recv.at[6], "gx", 1),
        push(cols_b.at[2], got_b.at[2], send.at[7], recv.at[7], "gx", -1),
        push(side_mask, left_mask, send.at[8], recv.at[8], "gx", 1),
    ]
    for start, wait in far:
        start()

    @pl.loop(quads // 2 + 1, quads - 1)
    def _(p):
        four_rows(p)

    for start, wait in far:
        wait()
    sides[...] = got_b[pl.ds(1, 2)].astype(f32)
    for s in (0, 1, ny + 2):
        widen(s)

    for dx in range(3):
        wide = cols[2] if dx == 2 else got_b[dx].astype(f32)
        for dy in range(3):
            moved = wide if dy == 0 else pltpu.roll(wide, half - dy, 1)
            column[pl.ds((dy * 3 + dx) * cz, cz), :] = moved.astype(bf16)
    got = dot(w1[...], column[...])
    edge[...] = jnp.maximum(got + b1, 0.0) * left_mask[pl.ds(0, 1), :]
    hidden_row(0, ((0, 0, 0),))

    @pl.loop(0, 2)
    def _(i):
        four_rows(i * (quads - 1))

    @pl.loop(0, quads)
    def _(p):
        for dy in range(3):
            spot = pl.ds(pl.multiple_of((p * 9 + dy * 3) * cz, cz), cz)
            pair = []
            for side in range(2):
                t = 4 * p + 2 * side + dy
                first = pltpu.roll(edge[...], lax.rem(half - t, half), 1)
                old = hid[spot, pl.ds(side * half, half)].astype(f32)
                pair.append(jnp.where(lane == 0, first, old).astype(bf16))
            for side in range(2):
                hid[spot, pl.ds(side * half, half)] = pair[side]
        got = dot(w2[...], hid[pl.ds(pl.multiple_of(p * 9 * cz, cz), 9 * cz), :])
        got = jnp.maximum(got + b2, 0.0).astype(bf16)
        feats[:, pl.ds(pl.multiple_of(p * nx, nx), nx)] = got
        wide = got.astype(f32)
        flat[pl.ds(2 * p, cz, stride=ny // 2), :] = wide[:, :half]
        flat[pl.ds(2 * p + 1, cz, stride=ny // 2), :] = wide[:, half:]

    for plane in range(z):
        piece = flat[pl.ds(plane * c * ny // 2, c * ny // 2), :]
        coarse[:, plane] = piece.reshape(c, ny // 2, half).astype(bf16)

    voxels = feats.shape[1]
    groups = part.shape[0] // PER
    chunk = spread.shape[0] // c

    @pl.loop(0, groups // chunk)
    def _(g):
        for plane in range(z):
            which = lax.rem(owners[pl.ds(plane, 1), :], PER) * SEG_DEV + segments[pl.ds(plane, 1), :]
            ids = lax.broadcasted_iota(jnp.int32, (PER * SEG_DEV, 1), 0)
            hot[...] = (ids == which).astype(f32).astype(bf16)
            owner = owners[pl.ds(plane, 1), :] // PER
            for a in range(chunk):
                on = (owner == g * chunk + a).astype(f32).astype(bf16)
                spread[pl.ds(a * c, c), :] = feats[pl.ds(plane * c, c), :] * on
            got = lax.dot_general(
                spread[...], hot[...], (((1,), (1,)), ((), ())), preferred_element_type=f32
            )
            if plane == 0:
                acc[...] = got
            else:
                acc[...] += got
        for a in range(chunk):
            for n in range(PER):
                part[(g * chunk + a) * PER + n] = acc[
                    pl.ds(a * c, c), pl.ds(n * SEG_DEV, SEG_DEV)
                ].astype(bf16)


def reduce_kernel(part, out, mine, got_x, got_y, send_x, recv_x, send_y, recv_y):
    f32, bf16 = jnp.float32, jnp.bfloat16
    x, y = lax.axis_index("gx"), lax.axis_index("gy")
    size_x, size_y = lax.axis_size("gx"), lax.axis_size("gy")
    barrier = pltpu.get_barrier_semaphore()
    for i in range(1, size_x):
        pl.semaphore_signal(
            barrier, inc=1, device_id={"gx": lax.rem(x + i, size_x)},
            device_id_type=pl.DeviceIdType.MESH,
        )
    for i in range(1, size_y):
        pl.semaphore_signal(
            barrier, inc=1, device_id={"gy": lax.rem(y + i, size_y)},
            device_id_type=pl.DeviceIdType.MESH,
        )
    pl.semaphore_wait(barrier, size_x + size_y - 2)

    def spread(axis, me, size, source, target, send, recv):
        copies = []
        for i in range(1, size):
            to = lax.rem(me + i, size)
            copy = pltpu.make_async_remote_copy(
                src_ref=source.at[to], dst_ref=target.at[i], send_sem=send.at[i],
                recv_sem=recv.at[i], device_id={axis: to},
                device_id_type=pl.DeviceIdType.MESH,
            )
            copy.start()
            copies.append(copy)
        for copy in copies:
            copy.wait()

    spread("gx", x, size_x, part, got_x, send_x, recv_x)
    total = part[x].astype(f32)
    for i in range(1, size_x):
        total = total + got_x[i].astype(f32)
    mine[...] = total.astype(bf16)
    spread("gy", y, size_y, mine, got_y, send_y, recv_y)
    sums = mine[y].astype(f32)
    for i in range(1, size_y):
        sums = sums + got_y[i].astype(f32)
    out[...] = sums * lax.rsqrt(jnp.mean(sums * sums, axis=0, keepdims=True) + 1e-05)


def per_device(volume, brick_mask, w1, b1, w2, b2, voxel_owner, voxel_segment):
    c, z, ny, nx = volume.shape
    bf16, f32 = jnp.bfloat16, jnp.float32
    half, cz = nx // 2, c * z
    size_x, size_y = lax.axis_size("gx"), lax.axis_size("gy")
    devices = size_x * size_y
    tall = jnp.repeat(brick_mask, BY, 0)
    mask = jnp.repeat(tall, BX, 1).astype(bf16)
    own_mask = jnp.repeat(tall, BX // 2, 1).astype(f32)
    own_side = jnp.pad(tall[:, -1], (1, half - ny - 1)).astype(f32)
    own_side = jnp.broadcast_to(own_side[None], (8, half))
    wt1 = w1.transpose(2, 3, 4, 0, 1).reshape(27, c, c)
    wt2 = w2[:, :, 0].transpose(2, 3, 0, 1).reshape(9, c, c)
    owner = voxel_owner.reshape(z, -1)
    segment = voxel_segment.reshape(z, -1)
    voxels = owner.shape[1]
    groups = devices // PER
    chunk = min(groups, 16)

    coarse, part = pl.pallas_call(
        block_kernel,
        out_shape=(
            jax.ShapeDtypeStruct((c, z, ny // 2, half), bf16),
            jax.ShapeDtypeStruct((devices, c, SEG_DEV), bf16),
        ),
        in_specs=[pl.BlockSpec(memory_space=pltpu.VMEM)] * 10,
        out_specs=[pl.BlockSpec(memory_space=pltpu.VMEM)] * 2,
        scratch_shapes=[
            pltpu.VMEM((2, c * ny, half), f32),
            pltpu.VMEM(((ny + 3) * 3 * cz, nx), bf16),
            pltpu.VMEM(((ny // 4 * 9 + 3) * cz, nx), bf16),
            pltpu.VMEM((cz, 9 * cz), bf16),
            pltpu.VMEM((cz, 9 * cz), bf16),
            pltpu.VMEM((cz, voxels), bf16),
            pltpu.VMEM((cz * ny // 2, half), f32),
            pltpu.VMEM((chunk * c, voxels), bf16),
            pltpu.VMEM((PER * SEG_DEV, voxels), bf16),
            pltpu.VMEM((chunk * c, PER * SEG_DEV), f32),
            pltpu.VMEM((3, cz, nx), bf16),
            pltpu.VMEM((3, cz, half), f32),
            pltpu.VMEM((3, cz, half), bf16),
            pltpu.VMEM((3, cz, half), bf16),
            pltpu.VMEM((2, cz, half), bf16),
            pltpu.VMEM((3, cz, half), bf16),
            pltpu.VMEM((2, cz, half), f32),
            pltpu.VMEM((9 * cz, half), bf16),
            pltpu.VMEM((ny + 8, half), f32),
            pltpu.VMEM((8, half), f32),
            pltpu.VMEM((8, half), f32),
            pltpu.VMEM((8, half), f32),
            pltpu.VMEM((cz, half), f32),
            pltpu.SemaphoreType.DMA((9,)),
            pltpu.SemaphoreType.DMA((9,)),
        ],
        compiler_params=pltpu.CompilerParams(
            collective_id=0, has_side_effects=True, vmem_limit_bytes=58 * 1024 * 1024
        ),
    )(volume, mask, wt1, wt2, b1[None], b2[None], own_mask, own_side, owner, segment)
    supervox = pl.pallas_call(
        reduce_kernel,
        out_shape=jax.ShapeDtypeStruct((c, SEG_DEV), f32),
        in_specs=[pl.BlockSpec(memory_space=pltpu.VMEM)],
        out_specs=pl.BlockSpec(memory_space=pltpu.VMEM),
        scratch_shapes=[
            pltpu.VMEM((size_y, c, SEG_DEV), bf16),
            pltpu.VMEM((size_x, size_y, c, SEG_DEV), bf16),
            pltpu.VMEM((size_y, c, SEG_DEV), bf16),
            pltpu.SemaphoreType.DMA((size_x,)),
            pltpu.SemaphoreType.DMA((size_x,)),
            pltpu.SemaphoreType.DMA((size_y,)),
            pltpu.SemaphoreType.DMA((size_y,)),
        ],
        compiler_params=pltpu.CompilerParams(
            collective_id=1, has_side_effects=True, vmem_limit_bytes=32 * 1024 * 1024
        ),
    )(part.reshape(size_x, size_y, c, SEG_DEV))
    return (coarse, supervox)


def solution(mesh):
    placed = (
        P(None, None, "gy", "gx"),
        P("gy", "gx"),
        P(),
        P(),
        P(),
        P(),
        P(("gx", "gy"), None),
        P(("gx", "gy")),
    )
    return jax.shard_map(
        per_device,
        mesh=mesh,
        in_specs=placed,
        out_specs=(P(None, None, "gy", "gx"), P(None, ("gx", "gy"))),
        check_vma=False,
    )
```
